32 devices in a mesh: space: 16 (over z, y, x), tm: 2 (over core).
Axes of the slice: x: 2, y: 2, z: 4, core: 2. Of those that a mesh axis runs over, the one named last changes fastest.
Arguments:
- right_side: float32 [64, 128, 512], P('tm', 'space'), may hold values from -70 to 70
- kappa_field: float32 [128, 512], P('space'), may hold values from 0.1 to 2
- land_mask: int32 [128, 512], P('space'), may hold values 0 or 1
- nugget: float32 [64], P('tm'), may hold values from 0.5 to 2
- time_band: float32 [5, 64], P(None, 'tm'), may hold values from -0.22 to 1.5, as said below
- taper_width: int32 [8], replicated, may hold values from 1 to 4, as said below
Outputs:
- solution_field: float32 [64, 128, 512], P('tm', 'space')
- residual: float32 [64, 128, 512], P('tm', 'space')
The draws below stay inside these ranges and needn't reach their ends.
Inputs may be any that keep to these rules, and one draw needn't show every extreme that they name: `time_band`: row 0 holds the diagonal at each hour; row l holds the coupling between hour t and hour t + l, zero where t + l is past the last hour. `taper_width`: some block has width 4 and some block has width 1.
All inputs are finite; a program needn't handle non-finite values. No bound on the sum of `land_mask` on one device may be relied on, other than what follows from the above.
Results may differ from the reference program's by a relative error of at most 0.034.
Values sent between devices are 32-bit elements; how exact they have to be, the bound alone decides.
A program may use at most 64 MiB of HBM per device.

```python
import math
import jax
import jax.numpy as jnp

NY = 512
TAPER_HOURS = 8
LAG = 4
ITERS = 2
NX = 128
NT = 64
TBLOCKS = 8


def draw_right_side(key, part):
    key = jax.random.fold_in(key, 11)
    subkeys = jax.random.split(key, 3)
    row_position = jnp.arange(NX, dtype=jnp.float32) / NX
    row_scale = jnp.exp(jax.random.uniform(subkeys[0], (NX,), jnp.float32, -1.1513, 1.1513))
    hour_scale = jnp.exp(jax.random.uniform(subkeys[1], (NT,), jnp.float32, -1.1513, 1.1513))
    trend_factor = jnp.exp(0.5493 * row_position)
    noise_values = jax.random.truncated_normal(subkeys[2], -4.0, 4.0, (NT, NX, NY), jnp.float32)
    combined = noise_values * (hour_scale[:, None, None] * (row_scale * trend_factor)[None, :, None])
    return jnp.clip(combined, -70.0, 70.0)


def draw_time_band(key, part):
    key = jax.random.fold_in(key, 23)
    subkeys = jax.random.split(key, 2)
    diagonal = jax.random.uniform(subkeys[0], (1, NT), jnp.float32, 1.0, 1.5)
    coupling = jax.random.uniform(subkeys[1], (LAG, NT), jnp.float32, -0.22, 0.22)
    hour_index = jnp.arange(NT, dtype=jnp.int32)[None, :]
    lag_index = jnp.arange(1, LAG + 1, dtype=jnp.int32)[:, None]
    coupling = jnp.where(hour_index + lag_index < NT, coupling, 0.0)
    return jnp.concatenate([diagonal, coupling], axis=0)


def draw_taper_width(key, part):
    key = jax.random.fold_in(key, 37)
    subkeys = jax.random.split(key, 2)
    widths = jax.random.randint(subkeys[0], (TBLOCKS,), 1, LAG + 1)
    ordering = jax.random.permutation(subkeys[1], TBLOCKS)
    widths = widths.at[ordering[0]].set(LAG)
    widths = widths.at[ordering[1]].set(1)
    return widths.astype(jnp.int32)


def plant(result, rng, smallest, largest):
    spot = [jax.random.randint(jax.random.fold_in(rng, axis), (), 0, length) for axis, length in enumerate(result.shape)]
    longest = result.shape.index(max(result.shape))
    next_to = spot[:longest] + [(spot[longest] + 1) % result.shape[longest]] + spot[longest + 1:]
    return result.at[tuple(spot)].set(smallest).at[tuple(next_to)].set(largest)


def block_scale(own_key, extent, cuts, low, high):
    level = 1.0
    for dim, blocks in cuts:
        draws = jax.random.uniform(jax.random.fold_in(jax.random.fold_in(own_key, 6), dim), (blocks,), jnp.float32, low / len(cuts), high / len(cuts))
        level = level * jnp.repeat(jnp.exp(draws), extent[dim] // blocks).reshape((-1,) + (1,) * (len(extent) - 1 - dim))
    return level


def setup_inputs(seed: int = 0) -> dict:
    seeds = jax.random.split(jax.random.key(seed), 7)
    return {
        "right_side": draw_right_side(jax.random.fold_in(seeds[6], 71), 0),
        "kappa_field": jnp.clip(jnp.exp(math.log(2.0) - 2.9957323 * jax.random.uniform(seeds[1], (NX, NY), jnp.float32) ** block_scale(seeds[1], (NX, NY), ((0, 16),), -0.2, 0.2)), 0.1, 2.0),
        "land_mask": plant((jax.random.randint(seeds[2], (NX, NY), 0, 4) < 3).astype(jnp.int32), jax.random.fold_in(seeds[2], 1), 0, 1),
        "nugget": jnp.clip(jnp.exp(math.log(2.0) - 1.3862944 * jax.random.uniform(seeds[3], (NT,), jnp.float32) ** block_scale(seeds[3], (NT,), ((0, 2),), -0.2, 0.2)), 0.5, 2.0),
        "time_band": draw_time_band(jax.random.fold_in(seeds[6], 71), 0),
        "taper_width": draw_taper_width(jax.random.fold_in(seeds[6], 71), 0),
    }


spde_scale = 0.0625


def screened_laplace(padded, kappa_rows):
    centre = padded[:, 1:-1, :]
    zero_column = jnp.zeros_like(centre[:, :, :1])
    across = jnp.concatenate([centre[:, :, 1:], zero_column], axis=2) + jnp.concatenate([zero_column, centre[:, :, :-1]], axis=2)
    return (kappa_rows + 4.0) * centre - (padded[:, 2:, :] + padded[:, :-2, :] + across)


def tapered_band(time_band, taper_width, first_hour):
    lag_count = time_band.shape[0] - 1
    hour_count = time_band.shape[1]
    lag_values = jnp.arange(1, lag_count + 1, dtype=jnp.int32).astype(jnp.float32)[:, None]
    block_ids = jnp.arange(taper_width.shape[0], dtype=jnp.int32)
    hour_block = (first_hour + jnp.arange(hour_count, dtype=jnp.int32)) // TAPER_HOURS
    hour_width = jnp.sum(jnp.where(hour_block[:, None] == block_ids[None, :], taper_width[None, :], 0), axis=1)
    taper_factor = jnp.maximum(1.0 - lag_values / (hour_width.astype(jnp.float32)[None, :] + 1.0), 0.0)
    return time_band[1:] * taper_factor


def temporal_band(padded, diagonal, upper_band, lower_band):
    lag_count = upper_band.shape[0]
    hour_count = upper_band.shape[1]
    summed = diagonal[:, None, None] * padded[lag_count:lag_count + hour_count]
    for lag_step in range(1, lag_count + 1):
        ahead = padded[lag_count + lag_step:lag_count + lag_step + hour_count]
        behind = padded[lag_count - lag_step:lag_count - lag_step + hour_count]
        earlier = lower_band[lag_step - 1, lag_count - lag_step:lag_count - lag_step + hour_count]
        summed = summed + upper_band[lag_step - 1][:, None, None] * ahead + earlier[:, None, None] * behind
    return summed


def reference(right_side, kappa_field, land_mask, nugget, time_band, taper_width):
    upper_band = tapered_band(time_band, taper_width, 0)
    lag_count = upper_band.shape[0]
    lower_band = jnp.pad(upper_band, ((0, 0), (lag_count, 0)))
    diagonal = time_band[0]
    land_weight = land_mask.astype(jnp.float32)

    def operate(grid_values):
        first_pass = screened_laplace(jnp.pad(grid_values, ((0, 0), (1, 1), (0, 0))), kappa_field)
        smoothed = spde_scale * screened_laplace(jnp.pad(first_pass, ((0, 0), (1, 1), (0, 0))), kappa_field)
        padded = jnp.pad(smoothed, ((lag_count, lag_count), (0, 0), (0, 0)))
        return temporal_band(padded, diagonal, upper_band, lower_band) + nugget[:, None, None] * (land_weight * grid_values)

    solution = jnp.zeros_like(right_side)
    residual = right_side
    direction = right_side
    norm_now = jnp.sum(residual * residual)
    for iteration in range(ITERS):
        applied = operate(direction)
        step_size = norm_now / jnp.sum(direction * applied)
        solution = solution + step_size * direction
        residual = residual - step_size * applied
        if iteration + 1 < ITERS:
            norm_next = jnp.sum(residual * residual)
            direction = residual + (norm_next / norm_now) * direction
            norm_now = norm_next
    return solution, residual
```

```python
import functools

import jax
import jax.numpy as jnp
from jax import lax
from jax.experimental import pallas as pl
from jax.experimental.pallas import tpu as pltpu
from jax.sharding import PartitionSpec as P

TAPER_HOURS = 8
LAG = 4
RIM = 2
LOW = 4

SPDE_SCALE = 0.0625
MESH = pl.DeviceIdType.MESH


def halo_offsets():
    return [(1, 0), (-1, 0), (1, 1), (1, -1), (-1, 1), (-1, -1), (0, 1), (0, -1)]


def kernel(
    ns,
    nt,
    right_ref,
    kappa_ref,
    mask_ref,
    nugget_ref,
    band_ref,
    taper_ref,
    q_out,
    w_ref,
    coef_ref,
    b_pad,
    b_rim,
    q_pad,
    q_rim,
    mixed,
    band,
    kappa_rim,
    sum_near,
    sum_far,
    local_sem,
    halo_send,
    halo_recv,
    aux_send,
    aux_recv,
    near_send,
    near_recv,
    far_send,
    far_recv,
):
    s = lax.axis_index("space")
    t = lax.axis_index("tm")
    hours = w_ref.shape[0]
    rows = w_ref.shape[1]
    cols = w_ref.shape[2]
    low = min(LOW, ns)
    near = low * nt
    far = ns // low

    load_b = pltpu.make_async_copy(right_ref, b_pad.at[pl.ds(LAG, hours)], local_sem.at[0])
    load_b.start()

    def near_partner(k):
        me = (s % low) * nt + t
        other = (me + k) % near
        return (s // low) * low + other // nt, other % nt

    def far_partner(k):
        other = (s // low + k) % far
        return other * low + s % low, t

    def exists(ds, dt):
        ok = None
        for pos, step, count in ((s, ds, ns), (t, dt, nt)):
            if step:
                here = pos < count - 1 if step > 0 else pos > 0
                ok = here if ok is None else jnp.logical_and(ok, here)
        return ok

    b_rim[...] = jnp.zeros_like(b_rim)
    q_rim[...] = jnp.zeros_like(q_rim)
    kappa_rim[...] = jnp.zeros_like(kappa_rim)
    edge = jnp.zeros((LAG, rows, cols), jnp.float32)
    for pad in (b_pad, q_pad):
        pad[0:LAG] = edge
        pad[LAG + hours : LAG + hours + LAG] = edge
    band[0:LAG] = jnp.zeros((LAG, 8, 128), jnp.float32)

    barrier = pltpu.get_barrier_semaphore()
    greeted = jnp.int32(near - 1 + far - 1)
    for ds, dt in halo_offsets():
        here = exists(ds, dt)
        greeted = greeted + here.astype(jnp.int32)

        @pl.when(here)
        def _():
            pl.semaphore_signal(barrier, inc=1, device_id=(s + ds, t + dt), device_id_type=MESH)

    for k in range(1, near):
        pl.semaphore_signal(barrier, inc=1, device_id=near_partner(k), device_id_type=MESH)
    for k in range(1, far):
        pl.semaphore_signal(barrier, inc=1, device_id=far_partner(k), device_id_type=MESH)

    lag_row = lax.broadcasted_iota(jnp.int32, (8, 128), 0)
    lag_value = lag_row.astype(jnp.float32)

    def fill_band(h, carry):
        width = taper_ref[(t * hours + h) // TAPER_HOURS].astype(jnp.float32)
        taper = jnp.maximum(1.0 - lag_value / (jnp.full((8, 128), width) + 1.0), 0.0)
        value = jnp.zeros((8, 128), jnp.float32)
        for l in range(LAG + 1):
            value = jnp.where(lag_row == l, band_ref[l, h], value)
        value = value * taper
        band[LAG + h] = jnp.where(lag_row == LAG + 1, nugget_ref[h], value)
        return carry

    lax.fori_loop(0, hours, fill_band, 0)

    load_b.wait()
    pl.semaphore_wait(barrier, greeted)

    row_of = {1: pl.ds(rows - RIM, RIM), -1: pl.ds(0, RIM)}
    hour_from = {0: pl.ds(LAG, hours), 1: pl.ds(hours, LAG), -1: pl.ds(LAG, LAG)}
    hour_to = {0: pl.ds(LAG, hours), 1: pl.ds(0, LAG), -1: pl.ds(LAG + hours, LAG)}

    def halo_copy(which, index, pad, rim):
        ds, dt = halo_offsets()[index]
        if ds:
            source = pad.at[hour_from[dt], row_of[ds]]
            target = rim.at[hour_to[dt], row_of[ds]]
        else:
            source = pad.at[hour_from[dt]]
            target = pad.at[hour_to[dt]]
        return pltpu.make_async_remote_copy(
            src_ref=source,
            dst_ref=target,
            send_sem=halo_send.at[which, index],
            recv_sem=halo_recv.at[which, index],
            device_id=(s + ds, t + dt),
            device_id_type=MESH,
        )

    def aux_copies():
        out = []
        for n, (ds, row) in enumerate(((1, rows - 1), (-1, 0))):
            out.append((
                ds,
                0,
                pltpu.make_async_remote_copy(
                    src_ref=kappa_ref.at[pl.ds(row, 1)],
                    dst_ref=kappa_rim.at[pl.ds(row, 1)],
                    send_sem=aux_send.at[n],
                    recv_sem=aux_recv.at[n],
                    device_id=(s + ds, t),
                    device_id_type=MESH,
                ),
            ))
        out.append((
            0,
            1,
            pltpu.make_async_remote_copy(
                src_ref=band.at[pl.ds(hours, LAG)],
                dst_ref=band.at[pl.ds(0, LAG)],
                send_sem=aux_send.at[2],
                recv_sem=aux_recv.at[2],
                device_id=(s, t + 1),
                device_id_type=MESH,
            ),
        ))
        return out

    def start_halo(which, pad, rim):
        for index, (ds, dt) in enumerate(halo_offsets()):

            @pl.when(exists(ds, dt))
            def _():
                halo_copy(which, index, pad, rim).start()

    def wait_halo(which, pad, rim, along_hours):
        for index, (ds, dt) in enumerate(halo_offsets()):
            if (ds == 0) == along_hours:

                @pl.when(exists(-ds, -dt))
                def _():
                    halo_copy(which, index, pad, rim).wait_recv()

    def drain_halo(which, pad, rim):
        for index, (ds, dt) in enumerate(halo_offsets()):

            @pl.when(exists(ds, dt))
            def _():
                halo_copy(which, index, pad, rim).wait_send()

    start_halo(0, b_pad, b_rim)
    for ds, dt, copy in aux_copies():

        @pl.when(exists(ds, dt))
        def _():
            copy.start()

    grid_row = lax.broadcasted_iota(jnp.int32, (rows, cols), 0)
    grid_col = lax.broadcasted_iota(jnp.int32, (rows, cols), 1)
    first_row = grid_row == 0
    last_row = grid_row == rows - 1
    first_col = grid_col == 0
    last_col = grid_col == cols - 1

    def coupling(h, row):
        return jnp.concatenate([band[h, pl.ds(row, 1), :]] * (cols // 128), axis=1)

    def along_time(field, h):
        total = coupling(LAG + h, 0) * field[LAG + h]
        for l in range(1, LAG + 1):
            total = (
                total
                + coupling(LAG + h, l) * field[LAG + h + l]
                + coupling(LAG + h - l, l) * field[LAG + h - l]
            )
        return total

    def laplace(x, rim, kappa4):
        above = pltpu.roll(jnp.where(last_row, rim, x), 1, 0)
        below = pltpu.roll(jnp.where(first_row, rim, x), rows - 1, 0)
        left = jnp.where(first_col, 0.0, pltpu.roll(x, 1, 1))
        right = jnp.where(last_col, 0.0, pltpu.roll(x, cols - 1, 1))
        return kappa4 * x - ((above + below) + (left + right))

    def mix_hours(pad):
        def step(h, carry):
            mixed[h] = along_time(pad, h)
            return carry

        lax.fori_loop(0, hours, step, 0, unroll=2)

    def image(pad, rim, h):
        x = mixed[h]
        x_rim = along_time(rim, h)
        kappa4 = kappa_ref[...] + 4.0
        kappa4_rim = kappa_rim[...] + 4.0
        inside = jnp.logical_or(
            jnp.logical_and(last_row, s > 0), jnp.logical_and(first_row, s < ns - 1)
        )
        y = laplace(x, x_rim, kappa4)
        y_rim = jnp.where(inside, laplace(x_rim, x, kappa4_rim), 0.0)
        z = laplace(y, y_rim, kappa4)
        weight = coupling(LAG + h, LAG + 1) * mask_ref[...].astype(jnp.float32)
        return SPDE_SCALE * z + weight * pad[LAG + h]

    def fold(x):
        out = x[:, :128]
        for c in range(128, cols, 128):
            out = out + x[:, c : c + 128]
        return out

    def start_sum(which, buffers, sends, recvs, me, size, partner):
        copies = []
        for k in range(1, size):
            copy = pltpu.make_async_remote_copy(
                src_ref=buffers.at[which, me],
                dst_ref=buffers.at[which, me],
                send_sem=sends.at[which, k],
                recv_sem=recvs.at[which, k],
                device_id=partner(k),
                device_id_type=MESH,
            )
            copy.start()
            copies.append(copy)
        return copies

    near_me = (s % low) * nt + t
    far_me = s // low

    def start_near(which, first, second):
        one = jnp.sum(first, axis=0, keepdims=True)
        two = jnp.sum(second, axis=0, keepdims=True)
        value = jnp.where(lag_row == 0, one, jnp.where(lag_row == 1, two, 0.0))
        sum_near[which, near_me] = value
        return start_sum(which, sum_near, near_send, near_recv, near_me, near, near_partner)

    def finish_near(which, copies):
        for copy in copies:
            copy.wait()
        total = sum_near[which, 0]
        for k in range(1, near):
            total = total + sum_near[which, k]
        return total

    def start_far(which, value):
        sum_far[which, far_me] = value
        return start_sum(which, sum_far, far_send, far_recv, far_me, far, far_partner)

    def finish_far(which, copies):
        for copy in copies:
            copy.wait()
        total = sum_far[which, 0]
        for k in range(1, far):
            total = total + sum_far[which, k]
        total = jnp.sum(total, axis=1, keepdims=True)
        return total[0:1, :], total[1:2, :]

    wait_halo(0, b_pad, b_rim, True)
    for ds, dt, copy in aux_copies():

        @pl.when(exists(-ds, -dt))
        def _():
            copy.wait_recv()

    mix_hours(b_pad)
    wait_halo(0, b_pad, b_rim, False)

    def first_step(h, carry):
        norm, product = carry
        value = image(b_pad, b_rim, h)
        q_pad[LAG + h] = value
        b = b_pad[LAG + h]
        return norm + fold(b * b), product + fold(b * value)

    zero = jnp.zeros((rows, 128), jnp.float32)
    norm, product = lax.fori_loop(0, hours, first_step, (zero, zero), unroll=2)

    start_halo(1, q_pad, q_rim)
    copies = start_near(0, norm, product)
    store_q = pltpu.make_async_copy(q_pad.at[pl.ds(LAG, hours)], q_out, local_sem.at[1])
    store_q.start()
    drain_halo(0, b_pad, b_rim)
    for ds, dt, copy in aux_copies():

        @pl.when(exists(ds, dt))
        def _():
            copy.wait_send()

    wait_halo(1, q_pad, q_rim, True)
    value = finish_near(0, copies)
    copies = start_far(0, value)
    mix_hours(q_pad)
    norm_0, product_0 = finish_far(0, copies)
    step_0 = norm_0 / product_0
    wait_halo(1, q_pad, q_rim, False)

    def second_step(h, carry):
        norm, product = carry
        q = q_pad[LAG + h]
        value = image(q_pad, q_rim, h)
        w_ref[h] = value
        left = b_pad[LAG + h] - step_0 * q
        left_image = q - step_0 * value
        return norm + fold(left * left), product + fold(left * left_image)

    norm, product = lax.fori_loop(0, hours, second_step, (zero, zero), unroll=2)
    copies = start_near(1, norm, product)
    drain_halo(1, q_pad, q_rim)
    store_q.wait()
    value = finish_near(1, copies)
    copies = start_far(1, value)
    norm_1, product_1 = finish_far(1, copies)

    ratio = norm_1 / norm_0
    step_1 = norm_1 / (product_1 - ratio * norm_1 / step_0)
    scale_1 = step_0 + step_1 * (1.0 + ratio)
    scale_2 = step_1 * step_0
    coef_ref[...] = jnp.where(lag_row == 0, scale_1, scale_2)


def body(ns, nt, right_side, kappa_field, land_mask, nugget, time_band, taper_width):
    hours, rows, cols = right_side.shape
    low = min(LOW, ns)
    near = low * nt
    far = ns // low
    padded = pltpu.VMEM((hours + 2 * LAG, rows, cols), jnp.float32)
    vmem = pl.BlockSpec(memory_space=pltpu.VMEM)
    smem = pl.BlockSpec(memory_space=pltpu.SMEM)
    hbm = pl.BlockSpec(memory_space=pl.ANY)
    field = jax.ShapeDtypeStruct(right_side.shape, jnp.float32)
    q, w, coef = pl.pallas_call(
        functools.partial(kernel, ns, nt),
        out_shape=(field, field, jax.ShapeDtypeStruct((8, 128), jnp.float32)),
        in_specs=[hbm, vmem, vmem, smem, smem, smem],
        out_specs=(hbm, vmem, vmem),
        scratch_shapes=[
            padded,
            padded,
            padded,
            padded,
            pltpu.VMEM((hours, rows, cols), jnp.float32),
            pltpu.VMEM((hours + LAG, 8, 128), jnp.float32),
            pltpu.VMEM((rows, cols), jnp.float32),
            pltpu.VMEM((2, near, 8, 128), jnp.float32),
            pltpu.VMEM((2, far, 8, 128), jnp.float32),
            pltpu.SemaphoreType.DMA((2,)),
            pltpu.SemaphoreType.DMA((2, 8)),
            pltpu.SemaphoreType.DMA((2, 8)),
            pltpu.SemaphoreType.DMA((3,)),
            pltpu.SemaphoreType.DMA((3,)),
            pltpu.SemaphoreType.DMA((2, near)),
            pltpu.SemaphoreType.DMA((2, near)),
            pltpu.SemaphoreType.DMA((2, far)),
            pltpu.SemaphoreType.DMA((2, far)),
        ],
        compiler_params=pltpu.CompilerParams(
            collective_id=0, has_side_effects=True, vmem_limit_bytes=32 * 1024 * 1024
        ),
        cost_estimate=pl.CostEstimate(
            flops=200 * right_side.size, bytes_accessed=12 * right_side.size, transcendentals=0
        ),
    )(right_side, kappa_field, land_mask, nugget, time_band, taper_width)
    scale_1 = coef[0, 0]
    scale_2 = coef[1, 0]
    return (
        scale_1 * right_side - scale_2 * q,
        right_side - scale_1 * q + scale_2 * w,
    )


def solution(mesh):
    return jax.shard_map(
        functools.partial(body, mesh.shape["space"], mesh.shape["tm"]),
        mesh=mesh,
        in_specs=(
            P("tm", "space", None),
            P("space", None),
            P("space", None),
            P("tm"),
            P(None, "tm"),
            P(),
        ),
        out_specs=(P("tm", "space", None), P("tm", "space", None)),
        check_vma=False,
    )
```

```python
import functools

import jax
import jax.numpy as jnp
from jax import lax
from jax.experimental import pallas as pl
from jax.experimental.pallas import tpu as pltpu
from jax.sharding import PartitionSpec as P

TAPER_HOURS = 8
LAG = 4
RIM = 2
LOW = 16

SPDE_SCALE = 0.0625
MESH = pl.DeviceIdType.MESH


def halo_offsets():
    return [(1, 0), (-1, 0), (1, 1), (1, -1), (-1, 1), (-1, -1), (0, 1), (0, -1)]


def kernel(
    ns,
    nt,
    right_ref,
    kappa_hbm,
    mask_hbm,
    nugget_ref,
    band_ref,
    taper_ref,
    q_out,
    w_ref,
    scale_1_ref,
    scale_2_ref,
    kappa_ref,
    mask_ref,
    b_pad,
    b_rim,
    q_pad,
    q_rim,
    mixed,
    band,
    kappa_rim,
    sum_near,
    sum_far,
    local_sem,
    halo_send,
    halo_recv,
    aux_send,
    aux_recv,
    near_send,
    near_recv,
    far_send,
    far_recv,
):
    s = lax.axis_index("space")
    t = lax.axis_index("tm")
    hours = w_ref.shape[0]
    rows = w_ref.shape[1]
    cols = w_ref.shape[2]
    low = min(LOW, ns)
    near = low * nt
    far = ns // low

    load_b = pltpu.make_async_copy(right_ref, b_pad.at[pl.ds(LAG, hours)], local_sem.at[0])
    load_b.start()
    load_kappa = pltpu.make_async_copy(kappa_hbm, kappa_ref, local_sem.at[2])
    load_kappa.start()
    load_mask = pltpu.make_async_copy(mask_hbm, mask_ref, local_sem.at[3])
    load_mask.start()

    def near_partner(k):
        me = (s % low) * nt + t
        other = (me + k) % near
        return (s // low) * low + other // nt, other % nt

    def far_partner(k):
        other = (s // low + k) % far
        return other * low + s % low, t

    def exists(ds, dt):
        ok = None
        for pos, step, count in ((s, ds, ns), (t, dt, nt)):
            if step:
                here = pos < count - 1 if step > 0 else pos > 0
                ok = here if ok is None else jnp.logical_and(ok, here)
        return ok

    b_rim[...] = jnp.zeros_like(b_rim)
    q_rim[...] = jnp.zeros_like(q_rim)
    kappa_rim[...] = jnp.zeros_like(kappa_rim)
    edge = jnp.zeros((LAG, rows, cols), jnp.float32)
    for pad in (b_pad, q_pad):
        pad[0:LAG] = edge
        pad[LAG + hours : LAG + hours + LAG] = edge
    band[0:LAG] = jnp.zeros((LAG, 8, 128), jnp.float32)

    barrier = pltpu.get_barrier_semaphore()
    greeted = jnp.int32(near - 1 + far - 1)
    for ds, dt in halo_offsets():
        here = exists(ds, dt)
        greeted = greeted + here.astype(jnp.int32)

        @pl.when(here)
        def _():
            pl.semaphore_signal(barrier, inc=1, device_id=(s + ds, t + dt), device_id_type=MESH)

    for k in range(1, near):
        pl.semaphore_signal(barrier, inc=1, device_id=near_partner(k), device_id_type=MESH)
    for k in range(1, far):
        pl.semaphore_signal(barrier, inc=1, device_id=far_partner(k), device_id_type=MESH)

    lag_row = lax.broadcasted_iota(jnp.int32, (8, 128), 0)
    lag_value = lag_row.astype(jnp.float32)

    def fill_band(h, carry):
        width = taper_ref[(t * hours + h) // TAPER_HOURS].astype(jnp.float32)
        taper = jnp.maximum(1.0 - lag_value / (jnp.full((8, 128), width) + 1.0), 0.0)
        value = jnp.zeros((8, 128), jnp.float32)
        for l in range(LAG + 1):
            value = jnp.where(lag_row == l, band_ref[l, h], value)
        value = value * taper
        band[LAG + h] = jnp.where(lag_row == LAG + 1, nugget_ref[h], value)
        return carry

    lax.fori_loop(0, hours, fill_band, 0)

    load_b.wait()
    load_kappa.wait()
    load_mask.wait()
    pl.semaphore_wait(barrier, greeted)

    row_of = {1: pl.ds(rows - RIM, RIM), -1: pl.ds(0, RIM)}
    hour_from = {0: pl.ds(LAG, hours), 1: pl.ds(hours, LAG), -1: pl.ds(LAG, LAG)}
    hour_to = {0: pl.ds(LAG, hours), 1: pl.ds(0, LAG), -1: pl.ds(LAG + hours, LAG)}

    def halo_copy(which, index, pad, rim):
        ds, dt = halo_offsets()[index]
        if ds:
            source = pad.at[hour_from[dt], row_of[ds]]
            target = rim.at[hour_to[dt], row_of[ds]]
        else:
            source = pad.at[hour_from[dt]]
            target = pad.at[hour_to[dt]]
        return pltpu.make_async_remote_copy(
            src_ref=source,
            dst_ref=target,
            send_sem=halo_send.at[which, index],
            recv_sem=halo_recv.at[which, index],
            device_id=(s + ds, t + dt),
            device_id_type=MESH,
        )

    def aux_copies():
        out = []
        for n, (ds, row) in enumerate(((1, rows - 1), (-1, 0))):
            out.append((
                ds,
                0,
                pltpu.make_async_remote_copy(
                    src_ref=kappa_ref.at[pl.ds(row, 1)],
                    dst_ref=kappa_rim.at[pl.ds(row, 1)],
                    send_sem=aux_send.at[n],
                    recv_sem=aux_recv.at[n],
                    device_id=(s + ds, t),
                    device_id_type=MESH,
                ),
            ))
        out.append((
            0,
            1,
            pltpu.make_async_remote_copy(
                src_ref=band.at[pl.ds(hours, LAG)],
                dst_ref=band.at[pl.ds(0, LAG)],
                send_sem=aux_send.at[2],
                recv_sem=aux_recv.at[2],
                device_id=(s, t + 1),
                device_id_type=MESH,
            ),
        ))
        return out

    def start_halo(which, pad, rim):
        for index, (ds, dt) in enumerate(halo_offsets()):

            @pl.when(exists(ds, dt))
            def _():
                halo_copy(which, index, pad, rim).start()

    def wait_halo(which, pad, rim, along_hours):
        for index, (ds, dt) in enumerate(halo_offsets()):
            if (ds == 0) == along_hours:

                @pl.when(exists(-ds, -dt))
                def _():
                    halo_copy(which, index, pad, rim).wait_recv()

    def drain_halo(which, pad, rim):
        for index, (ds, dt) in enumerate(halo_offsets()):

            @pl.when(exists(ds, dt))
            def _():
                halo_copy(which, index, pad, rim).wait_send()

    start_halo(0, b_pad, b_rim)
    for ds, dt, copy in aux_copies():

        @pl.when(exists(ds, dt))
        def _():
            copy.start()

    grid_row = lax.broadcasted_iota(jnp.int32, (rows, cols), 0)
    grid_col = lax.broadcasted_iota(jnp.int32, (rows, cols), 1)
    first_row = grid_row == 0
    last_row = grid_row == rows - 1
    first_col = grid_col == 0
    last_col = grid_col == cols - 1

    def coupling(h, row):
        return jnp.concatenate([band[h, pl.ds(row, 1), :]] * (cols // 128), axis=1)

    def along_time(field, h):
        total = coupling(LAG + h, 0) * field[LAG + h]
        for l in range(1, LAG + 1):
            total = (
                total
                + coupling(LAG + h, l) * field[LAG + h + l]
                + coupling(LAG + h - l, l) * field[LAG + h - l]
            )
        return total

    def laplace(x, rim, kappa4):
        above = pltpu.roll(jnp.where(last_row, rim, x), 1, 0)
        below = pltpu.roll(jnp.where(first_row, rim, x), rows - 1, 0)
        left = jnp.where(first_col, 0.0, pltpu.roll(x, 1, 1))
        right = jnp.where(last_col, 0.0, pltpu.roll(x, cols - 1, 1))
        return kappa4 * x - ((above + below) + (left + right))

    def mix_hours(pad):
        def step(h, carry):
            mixed[h] = along_time(pad, h)
            return carry

        lax.fori_loop(0, hours, step, 0, unroll=2)

    def image(pad, rim, h):
        x = mixed[h]
        x_rim = along_time(rim, h)
        kappa4 = kappa_ref[...] + 4.0
        kappa4_rim = kappa_rim[...] + 4.0
        inside = jnp.logical_or(
            jnp.logical_and(last_row, s > 0), jnp.logical_and(first_row, s < ns - 1)
        )
        y = laplace(x, x_rim, kappa4)
        y_rim = jnp.where(inside, laplace(x_rim, x, kappa4_rim), 0.0)
        z = laplace(y, y_rim, kappa4)
        weight = coupling(LAG + h, LAG + 1) * mask_ref[...].astype(jnp.float32)
        return SPDE_SCALE * z + weight * pad[LAG + h]

    def fold(x):
        out = x[:, :128]
        for c in range(128, cols, 128):
            out = out + x[:, c : c + 128]
        return out

    def whole(x):
        return jnp.sum(jnp.sum(x, axis=0, keepdims=True), axis=1, keepdims=True)

    def shift_of(norm, product):
        return jnp.where(norm > 0.0, jnp.clip(product / norm, 0.0, 64.0), 0.0)

    def packed(values):
        tile = jnp.zeros((8, 128), jnp.float32)
        for row, value in enumerate(values):
            tile = jnp.where(lag_row == row, value, tile)
        return tile

    def gather(tile, slots, sends, recvs, me, size, partner):
        slots[me] = tile
        copies = []
        for k in range(1, size):
            copy = pltpu.make_async_remote_copy(
                src_ref=slots.at[me],
                dst_ref=slots.at[me],
                send_sem=sends.at[k],
                recv_sem=recvs.at[k],
                device_id=partner(k),
                device_id_type=MESH,
            )
            copy.start()
            copies.append(copy)
        for copy in copies:
            copy.wait()

    def merged(slots, size, shift_from):
        parts = [[slots[k, row : row + 1, :] for row in range(7)] for k in range(size)]
        norm = sum(p[0] for p in parts)
        product = sum(p[1] for p in parts)
        shift = shift_from(norm, product)
        square = cross = image_sum = mutual = 0.0
        for bb, bq, ee, eb, ef, eq, own in parts:
            d = own - shift
            square = square + (ee + d * (2.0 * eb + d * bb))
            cross = cross + (eb + d * bb)
            image_sum = image_sum + (ef + d * (eq + d * bq))
            mutual = mutual + (eq + 2.0 * d * bq)
        return [norm, product, square, cross, image_sum, mutual, shift]

    wait_halo(0, b_pad, b_rim, True)
    for ds, dt, copy in aux_copies():

        @pl.when(exists(-ds, -dt))
        def _():
            copy.wait_recv()

    mix_hours(b_pad)
    wait_halo(0, b_pad, b_rim, False)

    def first_step(h, carry):
        norm, product = carry
        value = image(b_pad, b_rim, h)
        q_pad[LAG + h] = value
        b = b_pad[LAG + h]
        return norm + fold(b * b), product + fold(b * value)

    zero = jnp.zeros((rows, 128), jnp.float32)
    norm, product = lax.fori_loop(0, hours, first_step, (zero, zero), unroll=2)

    start_halo(1, q_pad, q_rim)
    store_q = pltpu.make_async_copy(q_pad.at[pl.ds(LAG, hours)], q_out, local_sem.at[1])
    store_q.start()
    drain_halo(0, b_pad, b_rim)
    for ds, dt, copy in aux_copies():

        @pl.when(exists(ds, dt))
        def _():
            copy.wait_send()

    norm = whole(norm)
    product = whole(product)
    shift = shift_of(norm, product)
    wait_halo(1, q_pad, q_rim, True)
    mix_hours(q_pad)
    wait_halo(1, q_pad, q_rim, False)

    def second_step(h, carry):
        square, cross, image_sum, mutual = carry
        b = b_pad[LAG + h]
        q = q_pad[LAG + h]
        value = image(q_pad, q_rim, h)
        w_ref[h] = value
        left = q - shift * b
        left_image = value - shift * q
        return (
            square + fold(left * left),
            cross + fold(left * b),
            image_sum + fold(left * left_image),
            mutual + fold(left * q + b * left_image),
        )

    sums = lax.fori_loop(0, hours, second_step, (zero,) * 4, unroll=2)
    tile = packed([norm, product] + [whole(x) for x in sums] + [shift])
    if far > 1:
        gather(tile, sum_near, near_send, near_recv, (s % low) * nt + t, near, near_partner)
        tile = packed(merged(sum_near, near, shift_of))
        gather(tile, sum_far, far_send, far_recv, s // low, far, far_partner)
        total = merged(sum_far, far, lambda x, y: y / x)
    else:
        gather(tile, sum_near, near_send, near_recv, (s % low) * nt + t, near, near_partner)
        total = merged(sum_near, near, lambda x, y: y / x)
    drain_halo(1, q_pad, q_rim)
    store_q.wait()

    norm, product, square, _, image_sum, _, _ = total
    step_0 = norm / product
    part = square / product
    ratio = step_0 * part
    step_1 = square / (image_sum - square * part)
    scale_1 = step_0 + step_1 * (1.0 + ratio)
    scale_2 = step_1 * step_0
    for scale, ref in ((scale_1, scale_1_ref), (scale_2, scale_2_ref)):
        ref[...] = jnp.broadcast_to(jnp.concatenate([scale] * (cols // 128), axis=1), (rows, cols))


def body(ns, nt, right_side, kappa_field, land_mask, nugget, time_band, taper_width):
    hours, rows, cols = right_side.shape
    low = min(LOW, ns)
    near = low * nt
    far = ns // low
    padded = pltpu.VMEM((hours + 2 * LAG, rows, cols), jnp.float32)
    vmem = pl.BlockSpec(memory_space=pltpu.VMEM)
    smem = pl.BlockSpec(memory_space=pltpu.SMEM)
    hbm = pl.BlockSpec(memory_space=pl.ANY)
    field = jax.ShapeDtypeStruct(right_side.shape, jnp.float32)
    plane = jax.ShapeDtypeStruct((rows, cols), jnp.float32)
    q, w, scale_1, scale_2 = pl.pallas_call(
        functools.partial(kernel, ns, nt),
        out_shape=(field, field, plane, plane),
        in_specs=[hbm, hbm, hbm, smem, smem, smem],
        out_specs=(hbm, vmem, vmem, vmem),
        scratch_shapes=[
            pltpu.VMEM((rows, cols), jnp.float32),
            pltpu.VMEM((rows, cols), jnp.int32),
            padded,
            padded,
            padded,
            padded,
            pltpu.VMEM((hours, rows, cols), jnp.float32),
            pltpu.VMEM((hours + LAG, 8, 128), jnp.float32),
            pltpu.VMEM((rows, cols), jnp.float32),
            pltpu.VMEM((near, 8, 128), jnp.float32),
            pltpu.VMEM((far, 8, 128), jnp.float32),
            pltpu.SemaphoreType.DMA((4,)),
            pltpu.SemaphoreType.DMA((2, 8)),
            pltpu.SemaphoreType.DMA((2, 8)),
            pltpu.SemaphoreType.DMA((3,)),
            pltpu.SemaphoreType.DMA((3,)),
            pltpu.SemaphoreType.DMA((near,)),
            pltpu.SemaphoreType.DMA((near,)),
            pltpu.SemaphoreType.DMA((far,)),
            pltpu.SemaphoreType.DMA((far,)),
        ],
        compiler_params=pltpu.CompilerParams(
            collective_id=0, has_side_effects=True, vmem_limit_bytes=60 * 1024 * 1024
        ),
        cost_estimate=pl.CostEstimate(
            flops=200 * right_side.size, bytes_accessed=12 * right_side.size, transcendentals=0
        ),
    )(right_side, kappa_field, land_mask, nugget, time_band, taper_width)
    return (
        scale_1 * right_side - scale_2 * q,
        right_side - scale_1 * q + scale_2 * w,
    )


def solution(mesh):
    return jax.shard_map(
        functools.partial(body, mesh.shape["space"], mesh.shape["tm"]),
        mesh=mesh,
        in_specs=(
            P("tm", "space", None),
            P("space", None),
            P("space", None),
            P("tm"),
            P(None, "tm"),
            P(),
        ),
        out_specs=(P("tm", "space", None), P("tm", "space", None)),
        check_vma=False,
    )
```

```python
import functools

import jax
import jax.numpy as jnp
from jax import lax
from jax.experimental import pallas as pl
from jax.experimental.pallas import tpu as pltpu
from jax.sharding import PartitionSpec as P

TAPER_HOURS = 8
LAG = 4
RIM = 2
LOW = 16
CHUNKS = 4

SPDE_SCALE = 0.0625
MESH = pl.DeviceIdType.MESH


def halo_offsets():
    return [(0, 1), (0, -1), (1, 1), (1, -1), (-1, 1), (-1, -1), (1, 0), (-1, 0)]


def kernel(
    ns,
    nt,
    right_ref,
    kappa_hbm,
    mask_hbm,
    nugget_ref,
    band_ref,
    taper_ref,
    q_out,
    w_ref,
    scale_1_ref,
    scale_2_ref,
    kappa_ref,
    mask_ref,
    b_pad,
    b_rim,
    q_pad,
    q_rim,
    mixed,
    band,
    kappa_rim,
    sum_near,
    sum_far,
    local_sem,
    halo_send,
    halo_recv,
    aux_send,
    aux_recv,
    near_send,
    near_recv,
    far_send,
    far_recv,
    chunk_send,
    chunk_recv,
):
    s = lax.axis_index("space")
    t = lax.axis_index("tm")
    hours = w_ref.shape[0]
    rows = w_ref.shape[1]
    cols = w_ref.shape[2]
    low = min(LOW, ns)
    near = low * nt
    far = ns // low
    size = hours // CHUNKS

    load_b = pltpu.make_async_copy(right_ref, b_pad.at[pl.ds(LAG, hours)], local_sem.at[0])
    load_b.start()
    load_kappa = pltpu.make_async_copy(kappa_hbm, kappa_ref, local_sem.at[2])
    load_kappa.start()
    load_mask = pltpu.make_async_copy(mask_hbm, mask_ref, local_sem.at[3])
    load_mask.start()

    def near_partner(k):
        me = (s % low) * nt + t
        other = (me + k) % near
        return (s // low) * low + other // nt, other % nt

    def far_partner(k):
        other = (s // low + k) % far
        return other * low + s % low, t

    def exists(ds, dt):
        ok = None
        for pos, step, count in ((s, ds, ns), (t, dt, nt)):
            if step:
                here = pos < count - 1 if step > 0 else pos > 0
                ok = here if ok is None else jnp.logical_and(ok, here)
        return ok

    b_rim[...] = jnp.zeros_like(b_rim)
    q_rim[...] = jnp.zeros_like(q_rim)
    kappa_rim[...] = jnp.zeros_like(kappa_rim)
    edge = jnp.zeros((LAG, rows, cols), jnp.float32)
    for pad in (b_pad, q_pad):
        pad[0:LAG] = edge
        pad[LAG + hours : LAG + hours + LAG] = edge
    band[0:LAG] = jnp.zeros((LAG, 8, 128), jnp.float32)

    barrier = pltpu.get_barrier_semaphore()
    greeted = jnp.int32(near - 1 + far - 1)
    for ds, dt in halo_offsets():
        here = exists(ds, dt)
        greeted = greeted + here.astype(jnp.int32)

        @pl.when(here)
        def _():
            pl.semaphore_signal(barrier, inc=1, device_id=(s + ds, t + dt), device_id_type=MESH)

    for k in range(1, near):
        pl.semaphore_signal(barrier, inc=1, device_id=near_partner(k), device_id_type=MESH)
    for k in range(1, far):
        pl.semaphore_signal(barrier, inc=1, device_id=far_partner(k), device_id_type=MESH)

    lag_row = lax.broadcasted_iota(jnp.int32, (8, 128), 0)
    lag_value = lag_row.astype(jnp.float32)

    def fill_band(h, carry):
        width = taper_ref[(t * hours + h) // TAPER_HOURS].astype(jnp.float32)
        taper = jnp.maximum(1.0 - lag_value / (jnp.full((8, 128), width) + 1.0), 0.0)
        value = jnp.zeros((8, 128), jnp.float32)
        for l in range(LAG + 1):
            value = jnp.where(lag_row == l, band_ref[l, h], value)
        value = value * taper
        band[LAG + h] = jnp.where(lag_row == LAG + 1, nugget_ref[h], value)
        return carry

    lax.fori_loop(0, hours, fill_band, 0)

    load_b.wait()
    load_kappa.wait()
    load_mask.wait()
    pl.semaphore_wait(barrier, greeted)

    row_of = {1: pl.ds(rows - RIM, RIM), -1: pl.ds(0, RIM)}
    hour_from = {0: pl.ds(LAG, hours), 1: pl.ds(hours, LAG), -1: pl.ds(LAG, LAG)}
    hour_to = {0: pl.ds(LAG, hours), 1: pl.ds(0, LAG), -1: pl.ds(LAG + hours, LAG)}

    def halo_copy(which, index, pad, rim):
        ds, dt = halo_offsets()[index]
        if ds:
            source = pad.at[hour_from[dt], row_of[ds]]
            target = rim.at[hour_to[dt], row_of[ds]]
        else:
            source = pad.at[hour_from[dt]]
            target = pad.at[hour_to[dt]]
        return pltpu.make_async_remote_copy(
            src_ref=source,
            dst_ref=target,
            send_sem=halo_send.at[which, index],
            recv_sem=halo_recv.at[which, index],
            device_id=(s + ds, t + dt),
            device_id_type=MESH,
        )

    def aux_copies():
        out = []
        for n, (ds, row) in enumerate(((1, rows - 1), (-1, 0))):
            out.append((
                ds,
                0,
                pltpu.make_async_remote_copy(
                    src_ref=kappa_ref.at[pl.ds(row, 1)],
                    dst_ref=kappa_rim.at[pl.ds(row, 1)],
                    send_sem=aux_send.at[n],
                    recv_sem=aux_recv.at[n],
                    device_id=(s + ds, t),
                    device_id_type=MESH,
                ),
            ))
        out.append((
            0,
            1,
            pltpu.make_async_remote_copy(
                src_ref=band.at[pl.ds(hours, LAG)],
                dst_ref=band.at[pl.ds(0, LAG)],
                send_sem=aux_send.at[2],
                recv_sem=aux_recv.at[2],
                device_id=(s, t + 1),
                device_id_type=MESH,
            ),
        ))
        return out

    def chunk_copy(which, side, chunk, pad, rim):
        ds = (1, -1)[side]
        span = pl.ds(LAG + chunk * size, size)
        return pltpu.make_async_remote_copy(
            src_ref=pad.at[span, row_of[ds]],
            dst_ref=rim.at[span, row_of[ds]],
            send_sem=chunk_send.at[which, side, chunk],
            recv_sem=chunk_recv.at[which, side, chunk],
            device_id=(s + ds, t),
            device_id_type=MESH,
        )

    def start_edges(which, pad, rim, along):
        for index, (ds, dt) in enumerate(halo_offsets()):
            if dt == along:

                @pl.when(exists(ds, dt))
                def _():
                    halo_copy(which, index, pad, rim).start()

    def wait_edges(which, pad, rim, along, strips):
        for index, (ds, dt) in enumerate(halo_offsets()):
            if dt == along and (ds != 0) == strips:

                @pl.when(exists(-ds, -dt))
                def _():
                    halo_copy(which, index, pad, rim).wait_recv()

    def start_chunk(which, chunk, pad, rim):
        for side, ds in enumerate((1, -1)):

            @pl.when(exists(ds, 0))
            def _():
                chunk_copy(which, side, chunk, pad, rim).start()

    def wait_chunk(which, chunk, pad, rim):
        for side, ds in enumerate((1, -1)):

            @pl.when(exists(-ds, 0))
            def _():
                chunk_copy(which, side, chunk, pad, rim).wait_recv()

    def drain_halo(which, pad, rim):
        for index, (ds, dt) in enumerate(halo_offsets()):
            if dt:

                @pl.when(exists(ds, dt))
                def _():
                    halo_copy(which, index, pad, rim).wait_send()

        for chunk in range(CHUNKS):
            for side, ds in enumerate((1, -1)):

                @pl.when(exists(ds, 0))
                def _():
                    chunk_copy(which, side, chunk, pad, rim).wait_send()

    start_edges(0, b_pad, b_rim, 1)
    start_edges(0, b_pad, b_rim, -1)
    for chunk in range(CHUNKS):
        start_chunk(0, chunk, b_pad, b_rim)
    for ds, dt, copy in aux_copies():

        @pl.when(exists(ds, dt))
        def _():
            copy.start()

    grid_row = lax.broadcasted_iota(jnp.int32, (rows, cols), 0)
    grid_col = lax.broadcasted_iota(jnp.int32, (rows, cols), 1)
    first_row = grid_row == 0
    last_row = grid_row == rows - 1
    first_col = grid_col == 0
    last_col = grid_col == cols - 1

    def coupling(h, row):
        return jnp.concatenate([band[h, pl.ds(row, 1), :]] * (cols // 128), axis=1)

    def along_time(field, h):
        total = coupling(LAG + h, 0) * field[LAG + h]
        for l in range(1, LAG + 1):
            total = (
                total
                + coupling(LAG + h, l) * field[LAG + h + l]
                + coupling(LAG + h - l, l) * field[LAG + h - l]
            )
        return total

    def laplace(x, rim, kappa4):
        above = pltpu.roll(jnp.where(last_row, rim, x), 1, 0)
        below = pltpu.roll(jnp.where(first_row, rim, x), rows - 1, 0)
        left = jnp.where(first_col, 0.0, pltpu.roll(x, 1, 1))
        right = jnp.where(last_col, 0.0, pltpu.roll(x, cols - 1, 1))
        return kappa4 * x - ((above + below) + (left + right))

    def mix_hours(pad, first, last):
        def step(h, carry):
            mixed[h] = along_time(pad, h)
            return carry

        lax.fori_loop(first, last, step, 0, unroll=2)

    def image(pad, rim, h):
        x = mixed[h]
        x_rim = along_time(rim, h)
        kappa4 = kappa_ref[...] + 4.0
        kappa4_rim = kappa_rim[...] + 4.0
        inside = jnp.logical_or(
            jnp.logical_and(last_row, s > 0), jnp.logical_and(first_row, s < ns - 1)
        )
        y = laplace(x, x_rim, kappa4)
        y_rim = jnp.where(inside, laplace(x_rim, x, kappa4_rim), 0.0)
        z = laplace(y, y_rim, kappa4)
        weight = coupling(LAG + h, LAG + 1) * mask_ref[...].astype(jnp.float32)
        return SPDE_SCALE * z + weight * pad[LAG + h]

    def fold(x):
        out = x[:, :128]
        for c in range(128, cols, 128):
            out = out + x[:, c : c + 128]
        return out

    def whole(x):
        return jnp.sum(jnp.sum(x, axis=0, keepdims=True), axis=1, keepdims=True)

    def shift_of(norm, product):
        return jnp.where(norm > 0.0, jnp.clip(product / norm, 0.0, 64.0), 0.0)

    def packed(values):
        tile = jnp.zeros((8, 128), jnp.float32)
        for row, value in enumerate(values):
            tile = jnp.where(lag_row == row, value, tile)
        return tile

    def gather(tile, slots, sends, recvs, me, size, partner):
        slots[me] = tile
        copies = []
        for k in range(1, size):
            copy = pltpu.make_async_remote_copy(
                src_ref=slots.at[me],
                dst_ref=slots.at[me],
                send_sem=sends.at[k],
                recv_sem=recvs.at[k],
                device_id=partner(k),
                device_id_type=MESH,
            )
            copy.start()
            copies.append(copy)
        for copy in copies:
            copy.wait()

    def merged(slots, size, shift_from):
        parts = [[slots[k, row : row + 1, :] for row in range(7)] for k in range(size)]
        norm = sum(p[0] for p in parts)
        product = sum(p[1] for p in parts)
        shift = shift_from(norm, product)
        square = cross = image_sum = mutual = 0.0
        for bb, bq, ee, eb, ef, eq, own in parts:
            d = own - shift
            square = square + (ee + d * (2.0 * eb + d * bb))
            cross = cross + (eb + d * bb)
            image_sum = image_sum + (ef + d * (eq + d * bq))
            mutual = mutual + (eq + 2.0 * d * bq)
        return [norm, product, square, cross, image_sum, mutual, shift]

    wait_edges(0, b_pad, b_rim, 1, False)
    wait_edges(0, b_pad, b_rim, -1, False)
    for ds, dt, copy in aux_copies():

        @pl.when(exists(-ds, -dt))
        def _():
            copy.wait_recv()

    mix_hours(b_pad, 0, hours)

    def first_step(h, carry):
        norm, product = carry
        value = image(b_pad, b_rim, h)
        q_pad[LAG + h] = value
        b = b_pad[LAG + h]
        return norm + fold(b * b), product + fold(b * value)

    zero = jnp.zeros((rows, 128), jnp.float32)
    norm, product = zero, zero
    wait_edges(0, b_pad, b_rim, 1, True)
    wait_chunk(0, 0, b_pad, b_rim)
    for chunk in range(CHUNKS):
        if chunk + 1 < CHUNKS:
            wait_chunk(0, chunk + 1, b_pad, b_rim)
        else:
            wait_edges(0, b_pad, b_rim, -1, True)
        norm, product = lax.fori_loop(
            chunk * size, (chunk + 1) * size, first_step, (norm, product), unroll=2
        )
        if chunk == 0:
            start_edges(1, q_pad, q_rim, -1)
        if chunk == CHUNKS - 1:
            start_edges(1, q_pad, q_rim, 1)
        start_chunk(1, chunk, q_pad, q_rim)

    store_q = pltpu.make_async_copy(q_pad.at[pl.ds(LAG, hours)], q_out, local_sem.at[1])
    store_q.start()
    drain_halo(0, b_pad, b_rim)
    for ds, dt, copy in aux_copies():

        @pl.when(exists(ds, dt))
        def _():
            copy.wait_send()

    norm = whole(norm)
    product = whole(product)
    shift = shift_of(norm, product)
    mix_hours(q_pad, size, hours - size)
    wait_edges(1, q_pad, q_rim, -1, False)
    mix_hours(q_pad, hours - size, hours)
    wait_edges(1, q_pad, q_rim, 1, False)
    mix_hours(q_pad, 0, size)

    def second_step(h, carry):
        square, cross, image_sum, mutual = carry
        b = b_pad[LAG + h]
        q = q_pad[LAG + h]
        value = image(q_pad, q_rim, h)
        w_ref[h] = value
        left = q - shift * b
        left_image = value - shift * q
        return (
            square + fold(left * left),
            cross + fold(left * b),
            image_sum + fold(left * left_image),
            mutual + fold(left * q + b * left_image),
        )

    sums = (zero,) * 4
    wait_chunk(1, 0, q_pad, q_rim)
    wait_chunk(1, 1, q_pad, q_rim)
    for chunk in list(range(1, CHUNKS)) + [0]:
        if chunk == 0:
            wait_edges(1, q_pad, q_rim, 1, True)
        elif chunk + 1 < CHUNKS:
            wait_chunk(1, chunk + 1, q_pad, q_rim)
        else:
            wait_edges(1, q_pad, q_rim, -1, True)
        sums = lax.fori_loop(chunk * size, (chunk + 1) * size, second_step, sums, unroll=2)
    tile = packed([norm, product] + [whole(x) for x in sums] + [shift])
    if far > 1:
        gather(tile, sum_near, near_send, near_recv, (s % low) * nt + t, near, near_partner)
        tile = packed(merged(sum_near, near, shift_of))
        gather(tile, sum_far, far_send, far_recv, s // low, far, far_partner)
        total = merged(sum_far, far, lambda x, y: y / x)
    else:
        gather(tile, sum_near, near_send, near_recv, (s % low) * nt + t, near, near_partner)
        total = merged(sum_near, near, lambda x, y: y / x)
    drain_halo(1, q_pad, q_rim)
    store_q.wait()

    norm, product, square, _, image_sum, _, _ = total
    step_0 = norm / product
    part = square / product
    ratio = step_0 * part
    step_1 = square / (image_sum - square * part)
    scale_1 = step_0 + step_1 * (1.0 + ratio)
    scale_2 = step_1 * step_0
    for scale, ref in ((scale_1, scale_1_ref), (scale_2, scale_2_ref)):
        ref[...] = jnp.broadcast_to(jnp.concatenate([scale] * (cols // 128), axis=1), (rows, cols))


def body(ns, nt, right_side, kappa_field, land_mask, nugget, time_band, taper_width):
    hours, rows, cols = right_side.shape
    low = min(LOW, ns)
    near = low * nt
    far = ns // low
    padded = pltpu.VMEM((hours + 2 * LAG, rows, cols), jnp.float32)
    vmem = pl.BlockSpec(memory_space=pltpu.VMEM)
    smem = pl.BlockSpec(memory_space=pltpu.SMEM)
    hbm = pl.BlockSpec(memory_space=pl.ANY)
    field = jax.ShapeDtypeStruct(right_side.shape, jnp.float32)
    plane = jax.ShapeDtypeStruct((rows, cols), jnp.float32)
    q, w, scale_1, scale_2 = pl.pallas_call(
        functools.partial(kernel, ns, nt),
        out_shape=(field, field, plane, plane),
        in_specs=[hbm, hbm, hbm, smem, smem, smem],
        out_specs=(hbm, vmem, vmem, vmem),
        scratch_shapes=[
            pltpu.VMEM((rows, cols), jnp.float32),
            pltpu.VMEM((rows, cols), jnp.int32),
            padded,
            padded,
            padded,
            padded,
            pltpu.VMEM((hours, rows, cols), jnp.float32),
            pltpu.VMEM((hours + LAG, 8, 128), jnp.float32),
            pltpu.VMEM((rows, cols), jnp.float32),
            pltpu.VMEM((near, 8, 128), jnp.float32),
            pltpu.VMEM((far, 8, 128), jnp.float32),
            pltpu.SemaphoreType.DMA((4,)),
            pltpu.SemaphoreType.DMA((2, 8)),
            pltpu.SemaphoreType.DMA((2, 8)),
            pltpu.SemaphoreType.DMA((3,)),
            pltpu.SemaphoreType.DMA((3,)),
            pltpu.SemaphoreType.DMA((near,)),
            pltpu.SemaphoreType.DMA((near,)),
            pltpu.SemaphoreType.DMA((far,)),
            pltpu.SemaphoreType.DMA((far,)),
            pltpu.SemaphoreType.DMA((2, 2, CHUNKS)),
            pltpu.SemaphoreType.DMA((2, 2, CHUNKS)),
        ],
        compiler_params=pltpu.CompilerParams(
            collective_id=0, has_side_effects=True, vmem_limit_bytes=60 * 1024 * 1024
        ),
        cost_estimate=pl.CostEstimate(
            flops=200 * right_side.size, bytes_accessed=12 * right_side.size, transcendentals=0
        ),
    )(right_side, kappa_field, land_mask, nugget, time_band, taper_width)
    return (
        scale_1 * right_side - scale_2 * q,
        right_side - scale_1 * q + scale_2 * w,
    )


def solution(mesh):
    return jax.shard_map(
        functools.partial(body, mesh.shape["space"], mesh.shape["tm"]),
        mesh=mesh,
        in_specs=(
            P("tm", "space", None),
            P("space", None),
            P("space", None),
            P("tm"),
            P(None, "tm"),
            P(),
        ),
        out_specs=(P("tm", "space", None), P("tm", "space", None)),
        check_vma=False,
    )
```

```python
import functools

import jax
import jax.numpy as jnp
from jax import lax
from jax.experimental import pallas as pl
from jax.experimental.pallas import tpu as pltpu
from jax.sharding import PartitionSpec as P

TAPER_HOURS = 8
LAG = 4
RIM = 2
LOW = 16
CHUNKS = 4

SPDE_SCALE = 0.0625
MESH = pl.DeviceIdType.MESH


def halo_offsets():
    return [(0, 1), (0, -1), (1, 1), (1, -1), (-1, 1), (-1, -1), (1, 0), (-1, 0)]


def kernel(
    ns,
    nt,
    right_ref,
    kappa_hbm,
    mask_hbm,
    nugget_ref,
    band_ref,
    taper_ref,
    q_out,
    w_ref,
    scale_1_ref,
    scale_2_ref,
    kappa_ref,
    mask_ref,
    b_pad,
    b_rim,
    q_pad,
    q_rim,
    mixed,
    band,
    kappa_rim,
    sum_near,
    sum_far,
    local_sem,
    halo_send,
    halo_recv,
    aux_send,
    aux_recv,
    near_send,
    near_recv,
    far_send,
    far_recv,
    chunk_send,
    chunk_recv,
):
    s = lax.axis_index("space")
    t = lax.axis_index("tm")
    hours = w_ref.shape[0]
    rows = w_ref.shape[1]
    cols = w_ref.shape[2]
    low = min(LOW, ns)
    near = low * nt
    far = ns // low
    size = hours // CHUNKS

    load_b = pltpu.make_async_copy(right_ref, b_pad.at[pl.ds(LAG, hours)], local_sem.at[0])
    load_b.start()
    load_kappa = pltpu.make_async_copy(kappa_hbm, kappa_ref, local_sem.at[2])
    load_kappa.start()
    load_mask = pltpu.make_async_copy(mask_hbm, mask_ref, local_sem.at[3])
    load_mask.start()

    def near_partner(k):
        me = (s % low) * nt + t
        other = (me + k) % near
        return (s // low) * low + other // nt, other % nt

    def far_partner(k):
        other = (s // low + k) % far
        return other * low + s % low, t

    def exists(ds, dt):
        ok = None
        for pos, step, count in ((s, ds, ns), (t, dt, nt)):
            if step:
                here = pos < count - 1 if step > 0 else pos > 0
                ok = here if ok is None else jnp.logical_and(ok, here)
        return ok

    b_rim[...] = jnp.zeros_like(b_rim)
    q_rim[...] = jnp.zeros_like(q_rim)
    kappa_rim[...] = jnp.zeros_like(kappa_rim)
    edge = jnp.zeros((LAG, rows, cols), jnp.float32)
    for pad in (b_pad, q_pad):
        pad[0:LAG] = edge
        pad[LAG + hours : LAG + hours + LAG] = edge
    band[0:LAG] = jnp.zeros((LAG, 8, 128), jnp.float32)

    barrier = pltpu.get_barrier_semaphore()
    greeted = jnp.int32(near - 1 + far - 1)
    for ds, dt in halo_offsets():
        here = exists(ds, dt)
        greeted = greeted + here.astype(jnp.int32)

        @pl.when(here)
        def _():
            pl.semaphore_signal(barrier, inc=1, device_id=(s + ds, t + dt), device_id_type=MESH)

    for k in range(1, near):
        pl.semaphore_signal(barrier, inc=1, device_id=near_partner(k), device_id_type=MESH)
    for k in range(1, far):
        pl.semaphore_signal(barrier, inc=1, device_id=far_partner(k), device_id_type=MESH)

    lag_row = lax.broadcasted_iota(jnp.int32, (8, 128), 0)
    lag_value = lag_row.astype(jnp.float32)

    def fill_band(h, carry):
        width = taper_ref[(t * hours + h) // TAPER_HOURS].astype(jnp.float32)
        taper = jnp.maximum(1.0 - lag_value / (jnp.full((8, 128), width) + 1.0), 0.0)
        value = jnp.zeros((8, 128), jnp.float32)
        for l in range(LAG + 1):
            value = jnp.where(lag_row == l, band_ref[l, h], value)
        value = value * taper
        band[LAG + h] = jnp.where(lag_row == LAG + 1, nugget_ref[h], value)
        return carry

    lax.fori_loop(0, hours, fill_band, 0)

    load_b.wait()
    load_kappa.wait()
    load_mask.wait()
    pl.semaphore_wait(barrier, greeted)

    row_of = {1: pl.ds(rows - RIM, RIM), -1: pl.ds(0, RIM)}
    hour_from = {0: pl.ds(LAG, hours), 1: pl.ds(hours, LAG), -1: pl.ds(LAG, LAG)}
    hour_to = {0: pl.ds(LAG, hours), 1: pl.ds(0, LAG), -1: pl.ds(LAG + hours, LAG)}

    def halo_copy(which, index, pad, rim):
        ds, dt = halo_offsets()[index]
        if ds:
            source = pad.at[hour_from[dt], row_of[ds]]
            target = rim.at[hour_to[dt], row_of[ds]]
        else:
            source = pad.at[hour_from[dt]]
            target = pad.at[hour_to[dt]]
        return pltpu.make_async_remote_copy(
            src_ref=source,
            dst_ref=target,
            send_sem=halo_send.at[which, index],
            recv_sem=halo_recv.at[which, index],
            device_id=(s + ds, t + dt),
            device_id_type=MESH,
        )

    def aux_copies():
        out = []
        for n, (ds, row) in enumerate(((1, rows - 1), (-1, 0))):
            out.append((
                ds,
                0,
                pltpu.make_async_remote_copy(
                    src_ref=kappa_ref.at[pl.ds(row, 1)],
                    dst_ref=kappa_rim.at[pl.ds(row, 1)],
                    send_sem=aux_send.at[n],
                    recv_sem=aux_recv.at[n],
                    device_id=(s + ds, t),
                    device_id_type=MESH,
                ),
            ))
        out.append((
            0,
            1,
            pltpu.make_async_remote_copy(
                src_ref=band.at[pl.ds(hours, LAG)],
                dst_ref=band.at[pl.ds(0, LAG)],
                send_sem=aux_send.at[2],
                recv_sem=aux_recv.at[2],
                device_id=(s, t + 1),
                device_id_type=MESH,
            ),
        ))
        return out

    def chunk_copy(which, side, chunk, pad, rim):
        ds = (1, -1)[side]
        span = pl.ds(LAG + chunk * size, size)
        return pltpu.make_async_remote_copy(
            src_ref=pad.at[span, row_of[ds]],
            dst_ref=rim.at[span, row_of[ds]],
            send_sem=chunk_send.at[which, side, chunk],
            recv_sem=chunk_recv.at[which, side, chunk],
            device_id=(s + ds, t),
            device_id_type=MESH,
        )

    def start_edges(which, pad, rim, along):
        for index, (ds, dt) in enumerate(halo_offsets()):
            if dt == along:

                @pl.when(exists(ds, dt))
                def _():
                    halo_copy(which, index, pad, rim).start()

    def wait_edges(which, pad, rim, along, strips):
        for index, (ds, dt) in enumerate(halo_offsets()):
            if dt == along and (ds != 0) == strips:

                @pl.when(exists(-ds, -dt))
                def _():
                    halo_copy(which, index, pad, rim).wait_recv()

    def start_chunk(which, chunk, pad, rim):
        for side, ds in enumerate((1, -1)):

            @pl.when(exists(ds, 0))
            def _():
                chunk_copy(which, side, chunk, pad, rim).start()

    def wait_chunk(which, chunk, pad, rim):
        for side, ds in enumerate((1, -1)):

            @pl.when(exists(-ds, 0))
            def _():
                chunk_copy(which, side, chunk, pad, rim).wait_recv()

    def drain_halo(which, pad, rim):
        for index, (ds, dt) in enumerate(halo_offsets()):
            if dt:

                @pl.when(exists(ds, dt))
                def _():
                    halo_copy(which, index, pad, rim).wait_send()

        for chunk in range(CHUNKS):
            for side, ds in enumerate((1, -1)):

                @pl.when(exists(ds, 0))
                def _():
                    chunk_copy(which, side, chunk, pad, rim).wait_send()

    start_edges(0, b_pad, b_rim, 1)
    start_edges(0, b_pad, b_rim, -1)
    for chunk in range(CHUNKS):
        start_chunk(0, chunk, b_pad, b_rim)
    for ds, dt, copy in aux_copies():

        @pl.when(exists(ds, dt))
        def _():
            copy.start()

    grid_row = lax.broadcasted_iota(jnp.int32, (rows, cols), 0)
    grid_col = lax.broadcasted_iota(jnp.int32, (rows, cols), 1)
    first_row = grid_row == 0
    last_row = grid_row == rows - 1
    first_col = grid_col == 0
    last_col = grid_col == cols - 1

    def coupling(h, row):
        return jnp.concatenate([band[h, pl.ds(row, 1), :]] * (cols // 128), axis=1)

    def along_time(field, h):
        total = coupling(LAG + h, 0) * field[LAG + h]
        for l in range(1, LAG + 1):
            total = (
                total
                + coupling(LAG + h, l) * field[LAG + h + l]
                + coupling(LAG + h - l, l) * field[LAG + h - l]
            )
        return total

    def laplace(x, rim, kappa4):
        above = pltpu.roll(jnp.where(last_row, rim, x), 1, 0)
        below = pltpu.roll(jnp.where(first_row, rim, x), rows - 1, 0)
        left = jnp.where(first_col, 0.0, pltpu.roll(x, 1, 1))
        right = jnp.where(last_col, 0.0, pltpu.roll(x, cols - 1, 1))
        return kappa4 * x - ((above + below) + (left + right))

    def mix_hours(pad, first, last):
        def step(h, carry):
            mixed[h] = along_time(pad, h)
            return carry

        lax.fori_loop(first, last, step, 0, unroll=2)

    def image(pad, rim, h):
        x = mixed[h]
        x_rim = along_time(rim, h)
        kappa4 = kappa_ref[...] + 4.0
        kappa4_rim = kappa_rim[...] + 4.0
        inside = jnp.logical_or(
            jnp.logical_and(last_row, s > 0), jnp.logical_and(first_row, s < ns - 1)
        )
        y = laplace(x, x_rim, kappa4)
        y_rim = jnp.where(inside, laplace(x_rim, x, kappa4_rim), 0.0)
        z = laplace(y, y_rim, kappa4)
        weight = coupling(LAG + h, LAG + 1) * mask_ref[...].astype(jnp.float32)
        return SPDE_SCALE * z + weight * pad[LAG + h]

    def fold(x):
        out = x[:, :128]
        for c in range(128, cols, 128):
            out = out + x[:, c : c + 128]
        return out

    def whole(x):
        return jnp.sum(jnp.sum(x, axis=0, keepdims=True), axis=1, keepdims=True)

    def shift_of(norm, product):
        return jnp.where(norm > 0.0, jnp.clip(product / norm, 0.0, 64.0), 0.0)

    def packed(values):
        tile = jnp.zeros((8, 128), jnp.float32)
        for row, value in enumerate(values):
            tile = jnp.where(lag_row == row, value, tile)
        return tile

    def gather(tile, slots, sends, recvs, me, size, partner):
        slots[me] = tile
        copies = []
        for k in range(1, size):
            copy = pltpu.make_async_remote_copy(
                src_ref=slots.at[me],
                dst_ref=slots.at[me],
                send_sem=sends.at[k],
                recv_sem=recvs.at[k],
                device_id=partner(k),
                device_id_type=MESH,
            )
            copy.start()
            copies.append(copy)
        for copy in copies:
            copy.wait()

    def merged(slots, size, shift_from):
        parts = [[slots[k, row : row + 1, :] for row in range(7)] for k in range(size)]
        norm = sum(p[0] for p in parts)
        product = sum(p[1] for p in parts)
        shift = shift_from(norm, product)
        square = cross = image_sum = mutual = 0.0
        for bb, bq, ee, eb, ef, eq, own in parts:
            d = own - shift
            square = square + (ee + d * (2.0 * eb + d * bb))
            cross = cross + (eb + d * bb)
            image_sum = image_sum + (ef + d * (eq + d * bq))
            mutual = mutual + (eq + 2.0 * d * bq)
        return [norm, product, square, cross, image_sum, mutual, shift]

    wait_edges(0, b_pad, b_rim, 1, False)
    wait_edges(0, b_pad, b_rim, -1, False)
    for ds, dt, copy in aux_copies():

        @pl.when(exists(-ds, -dt))
        def _():
            copy.wait_recv()

    mix_hours(b_pad, 0, hours)

    def first_step(h, carry):
        norm, product = carry
        value = image(b_pad, b_rim, h)
        q_pad[LAG + h] = value
        b = b_pad[LAG + h]
        return norm + fold(b * b), product + fold(b * value)

    zero = jnp.zeros((rows, 128), jnp.float32)
    norm, product = zero, zero
    wait_edges(0, b_pad, b_rim, 1, True)
    wait_chunk(0, 0, b_pad, b_rim)
    for chunk in range(CHUNKS):
        if chunk + 1 < CHUNKS:
            wait_chunk(0, chunk + 1, b_pad, b_rim)
        else:
            wait_edges(0, b_pad, b_rim, -1, True)
        norm, product = lax.fori_loop(
            chunk * size, (chunk + 1) * size, first_step, (norm, product), unroll=4
        )
        if chunk == 0:
            start_edges(1, q_pad, q_rim, -1)
        if chunk == CHUNKS - 1:
            start_edges(1, q_pad, q_rim, 1)
        start_chunk(1, chunk, q_pad, q_rim)

    store_q = pltpu.make_async_copy(q_pad.at[pl.ds(LAG, hours)], q_out, local_sem.at[1])
    store_q.start()
    drain_halo(0, b_pad, b_rim)
    for ds, dt, copy in aux_copies():

        @pl.when(exists(ds, dt))
        def _():
            copy.wait_send()

    norm = whole(norm)
    product = whole(product)
    shift = shift_of(norm, product)
    mix_hours(q_pad, size, hours - size)
    wait_edges(1, q_pad, q_rim, -1, False)
    mix_hours(q_pad, hours - size, hours)
    wait_edges(1, q_pad, q_rim, 1, False)
    mix_hours(q_pad, 0, size)

    def second_step(h, carry):
        square, cross, image_sum, mutual = carry
        b = b_pad[LAG + h]
        q = q_pad[LAG + h]
        value = image(q_pad, q_rim, h)
        w_ref[h] = value
        left = q - shift * b
        left_image = value - shift * q
        return (
            square + fold(left * left),
            cross + fold(left * b),
            image_sum + fold(left * left_image),
            mutual + fold(left * q + b * left_image),
        )

    sums = (zero,) * 4
    wait_chunk(1, 0, q_pad, q_rim)
    wait_chunk(1, 1, q_pad, q_rim)
    for chunk in list(range(1, CHUNKS)) + [0]:
        if chunk == 0:
            wait_edges(1, q_pad, q_rim, 1, True)
        elif chunk + 1 < CHUNKS:
            wait_chunk(1, chunk + 1, q_pad, q_rim)
        else:
            wait_edges(1, q_pad, q_rim, -1, True)
        sums = lax.fori_loop(chunk * size, (chunk + 1) * size, second_step, sums, unroll=4)
    tile = packed([norm, product] + [whole(x) for x in sums] + [shift])
    if far > 1:
        gather(tile, sum_near, near_send, near_recv, (s % low) * nt + t, near, near_partner)
        tile = packed(merged(sum_near, near, shift_of))
        gather(tile, sum_far, far_send, far_recv, s // low, far, far_partner)
        total = merged(sum_far, far, lambda x, y: y / x)
    else:
        gather(tile, sum_near, near_send, near_recv, (s % low) * nt + t, near, near_partner)
        total = merged(sum_near, near, lambda x, y: y / x)
    drain_halo(1, q_pad, q_rim)
    store_q.wait()

    norm, product, square, _, image_sum, _, _ = total
    step_0 = norm / product
    part = square / product
    ratio = step_0 * part
    step_1 = square / (image_sum - square * part)
    scale_1 = step_0 + step_1 * (1.0 + ratio)
    scale_2 = step_1 * step_0
    for scale, ref in ((scale_1, scale_1_ref), (scale_2, scale_2_ref)):
        ref[...] = jnp.broadcast_to(jnp.concatenate([scale] * (cols // 128), axis=1), (rows, cols))


def body(ns, nt, right_side, kappa_field, land_mask, nugget, time_band, taper_width):
    hours, rows, cols = right_side.shape
    low = min(LOW, ns)
    near = low * nt
    far = ns // low
    padded = pltpu.VMEM((hours + 2 * LAG, rows, cols), jnp.float32)
    vmem = pl.BlockSpec(memory_space=pltpu.VMEM)
    smem = pl.BlockSpec(memory_space=pltpu.SMEM)
    hbm = pl.BlockSpec(memory_space=pl.ANY)
    field = jax.ShapeDtypeStruct(right_side.shape, jnp.float32)
    plane = jax.ShapeDtypeStruct((rows, cols), jnp.float32)
    q, w, scale_1, scale_2 = pl.pallas_call(
        functools.partial(kernel, ns, nt),
        out_shape=(field, field, plane, plane),
        in_specs=[hbm, hbm, hbm, smem, smem, smem],
        out_specs=(hbm, vmem, vmem, vmem),
        scratch_shapes=[
            pltpu.VMEM((rows, cols), jnp.float32),
            pltpu.VMEM((rows, cols), jnp.int32),
            padded,
            padded,
            padded,
            padded,
            pltpu.VMEM((hours, rows, cols), jnp.float32),
            pltpu.VMEM((hours + LAG, 8, 128), jnp.float32),
            pltpu.VMEM((rows, cols), jnp.float32),
            pltpu.VMEM((near, 8, 128), jnp.float32),
            pltpu.VMEM((far, 8, 128), jnp.float32),
            pltpu.SemaphoreType.DMA((4,)),
            pltpu.SemaphoreType.DMA((2, 8)),
            pltpu.SemaphoreType.DMA((2, 8)),
            pltpu.SemaphoreType.DMA((3,)),
            pltpu.SemaphoreType.DMA((3,)),
            pltpu.SemaphoreType.DMA((near,)),
            pltpu.SemaphoreType.DMA((near,)),
            pltpu.SemaphoreType.DMA((far,)),
            pltpu.SemaphoreType.DMA((far,)),
            pltpu.SemaphoreType.DMA((2, 2, CHUNKS)),
            pltpu.SemaphoreType.DMA((2, 2, CHUNKS)),
        ],
        compiler_params=pltpu.CompilerParams(
            collective_id=0, has_side_effects=True, vmem_limit_bytes=60 * 1024 * 1024
        ),
        cost_estimate=pl.CostEstimate(
            flops=200 * right_side.size, bytes_accessed=12 * right_side.size, transcendentals=0
        ),
    )(right_side, kappa_field, land_mask, nugget, time_band, taper_width)
    return (
        scale_1 * right_side - scale_2 * q,
        right_side - scale_1 * q + scale_2 * w,
    )


def solution(mesh):
    return jax.shard_map(
        functools.partial(body, mesh.shape["space"], mesh.shape["tm"]),
        mesh=mesh,
        in_specs=(
            P("tm", "space", None),
            P("space", None),
            P("space", None),
            P("tm"),
            P(None, "tm"),
            P(),
        ),
        out_specs=(P("tm", "space", None), P("tm", "space", None)),
        check_vma=False,
    )
```
